32 devices in a mesh: clips: 2 (over x), patch: 8 (over z, y), head: 2 (over core).
Axes of the slice: x: 2, y: 2, z: 4, core: 2. Of those that a mesh axis runs over, the one named last changes fastest.
Arguments:
- tokens: bfloat16 [4096, 3072], P(('clips', 'patch', 'head')), parts along dimension 0, may hold values from -6 to 6
- stale_kv: bfloat16 [4096, 2, 1536], P(('clips', 'patch'), None, 'head'), parts along dimension 0, may hold values from -6 to 6
- qkv_weight: bfloat16 [3072, 3, 1536], P(None, None, 'head'), may hold values from -0.109375 to 0.109375
- out_weight: bfloat16 [1536, 3072], P('head'), may hold values from -3 to 3
- modulation: float32 [2, 3, 3072], replicated, may hold values from -2 to 2
Outputs:
- next_tokens: bfloat16 [4096, 3072], P(('clips', 'patch', 'head')), parts along dimension 0
- kv_cache: bfloat16 [4096, 2, 1536], P(('clips', 'patch'), None, 'head'), parts along dimension 0
The draws below stay inside these ranges and needn't reach their ends.
There are 2 independent parts, one for each index of `clips`. The reference program is written for one: setup_inputs(seed, part) draws one part's arguments, and reference() takes and returns one part's arrays. A program takes and returns all parts, laid end to end along the dimension named above; an argument that names none is the same for every part. Nothing has to cross between parts.
All inputs are finite; a program needn't handle non-finite values.
Results may differ from the reference program's by a relative error of at most 0.014.
Values may be sent and summed in bfloat16 or wider, within the bound.
A program may use at most 192 MiB of HBM per device.

```python
import jax
import jax.numpy as jnp
from jax import lax

D = 3072
HEADS = 12
HD = 128
STEPS = 2
TOK_DEV = 128
TOKENS = 2048
N_PATCH = 8
N_HEAD = 2


def levels(stream_key, shape, shards, smallest, top_value):
    loudness, own = 1.0, jax.random.fold_in(stream_key, 6)
    for position, shards_of in shards:
        heights = jnp.exp(jax.random.uniform(jax.random.fold_in(own, position), (shards_of,), jnp.float32, smallest / len(shards), top_value / len(shards)))
        loudness = loudness * jnp.repeat(heights, shape[position] // shards_of).reshape([-1 if axis == position else 1 for axis in range(len(shape))])
    return loudness


def centred(own_key, shape, width, bound, shards=(), held_as=jnp.bfloat16):
    entries = width * jax.random.normal(own_key, shape, jnp.float32)
    if shards:
        entries = entries * levels(own_key, shape, shards, -0.22, 0.18)
    return jnp.clip(entries, -bound, bound).astype(held_as)


def setup_inputs(seed: int = 0, part: int = 0) -> dict:
    seeds = jax.random.split(jax.random.key(seed), 6)
    part_splits = jax.random.split(jax.random.fold_in(seeds[5], part), 6)
    return {
        "tokens": centred(part_splits[0], (TOKENS, D), 1.0, 6.0, ((0, 16),)),
        "stale_kv": centred(part_splits[1], (TOKENS, 2, HEADS * HD), 1.0, 6.0, ((0, 8), (2, 2))),
        "qkv_weight": centred(seeds[2], (D, 3, HEADS * HD), D ** -0.5, 0.109375, ((2, 2),)),
        "out_weight": centred(seeds[3], (HEADS * HD, D), 4 ** -0.5, 3.0, ((0, 2),)),
        "modulation": centred(seeds[4], (STEPS, 3, D), 0.5, 2.0, (), jnp.float32),
    }


epsilon = 1e-06

def modulate(state, shift_scale):
    values = state.astype(jnp.float32)
    centre = lax.optimization_barrier(jnp.mean(values, axis=-1, keepdims=True))
    spread = lax.optimization_barrier(jnp.mean(jnp.square(values - centre), axis=-1, keepdims=True))
    normed = (values - centre) * lax.rsqrt(spread + epsilon)
    return (normed * (1.0 + shift_scale[0]) + shift_scale[1]).astype(jnp.bfloat16)

def rms_heads(values):
    return values * lax.rsqrt(lax.optimization_barrier(jnp.mean(jnp.square(values), axis=-1, keepdims=True)) + epsilon)

def project(state, weights, shift_scale, head_size):
    hidden = modulate(state, shift_scale)
    row_count = state.shape[0]
    projected = jnp.dot(hidden, weights.reshape(weights.shape[0], -1), preferred_element_type=jnp.float32)
    separated = projected.reshape(row_count, 3, -1, head_size)
    queries = (rms_heads(separated[:, 0]) * head_size ** (-0.5)).astype(jnp.bfloat16)
    key_heads = rms_heads(separated[:, 1]).astype(jnp.bfloat16).reshape(row_count, -1)
    value_heads = separated[:, 2].astype(jnp.bfloat16).reshape(row_count, -1)
    return (queries, jnp.stack([key_heads, value_heads], axis=1))

def attend(queries, pairs):
    row_count = pairs.shape[0]
    head_count = queries.shape[1]
    head_size = queries.shape[2]
    key_heads = pairs[:, 0].reshape(row_count, head_count, head_size).astype(jnp.float32)
    value_heads = pairs[:, 1].reshape(row_count, head_count, head_size).astype(jnp.float32)
    scores = jnp.einsum('qhd,khd->qhk', queries.astype(jnp.float32), key_heads)
    exponent = jnp.exp(scores)
    probabilities = exponent.astype(jnp.bfloat16).astype(jnp.float32)
    numerator = jnp.einsum('qhk,khd->qhd', probabilities, value_heads)
    return (numerator, lax.optimization_barrier(jnp.sum(exponent, axis=-1)))

def reference(tokens, stale_kv, qkv_weight, out_weight, modulation):
    group_rows = TOK_DEV * N_HEAD
    state = tokens
    previous = stale_kv
    fresh_pairs = stale_kv
    for step_index in range(STEPS):
        shift_scale = modulation[step_index]
        queries, fresh_pairs = project(state, qkv_weight, shift_scale, HD)

        def patch_output(patch_index):
            offset = patch_index * group_rows
            local_queries = lax.dynamic_slice_in_dim(queries, offset, group_rows, 0)
            own_pairs = lax.dynamic_slice_in_dim(fresh_pairs, offset, group_rows, 0)
            merged = lax.dynamic_update_slice_in_dim(previous, own_pairs, offset, 0)
            numerator, denominator = attend(local_queries, merged)
            return (numerator / denominator[..., None]).astype(jnp.bfloat16).reshape(group_rows, -1)
        outputs = lax.map(patch_output, jnp.arange(N_PATCH, dtype=jnp.int32)).reshape(TOKENS, -1)
        branch = jnp.dot(outputs, out_weight, preferred_element_type=jnp.float32)
        state = (state.astype(jnp.float32) + (1.0 + shift_scale[2]) * branch).astype(jnp.bfloat16)
        previous = fresh_pairs
    return (state, fresh_pairs)
```

```python
import functools

import jax
import jax.numpy as jnp
from jax import lax
from jax.experimental import pallas as pl
from jax.experimental.pallas import tpu as pltpu
from jax.sharding import PartitionSpec as P

HD = 128
STEPS = 2
EPS = 1e-06
MESH = pl.DeviceIdType.MESH
F32, BF16 = jnp.float32, jnp.bfloat16


def kernel(
    lines,
    tokens_ref,
    stale_ref,
    wqkv_hbm,
    wout_hbm,
    mod_ref,
    next_ref,
    cache_hbm,
    wqkv,
    wout,
    kv,
    last_kv,
    hidden,
    q_own,
    q_peer,
    acc,
    num_out,
    num_in,
    den_out,
    den_in,
    attended,
    part_out,
    part_in,
    state,
    load_sem,
    kv_send,
    kv_recv,
    hid_sem,
    q_sem,
    num_sem,
    den_sem,
    part_sem,
):
    patch, head = lax.axis_index("patch"), lax.axis_index("head")
    a, b = patch // 2, patch % 2
    rows = tokens_ref.shape[0]
    heads = q_own.shape[1]
    size = q_own.shape[2]
    left = {"patch": patch - 2, "head": head}
    right = {"patch": patch + 2, "head": head}
    partner = {"patch": a * 2 + (1 - b), "head": head}
    core = {"patch": patch, "head": 1 - head}
    has_left, has_right = a > 0, a < lines - 1

    loads = [
        pltpu.make_async_copy(wqkv_hbm.at[i], wqkv.at[i], load_sem.at[i]) for i in range(3)
    ]
    loads.append(pltpu.make_async_copy(stale_ref, kv.at[0, a], load_sem.at[3]))
    loads.append(pltpu.make_async_copy(wout_hbm, wout, load_sem.at[4]))

    barrier = pltpu.get_barrier_semaphore()
    pl.semaphore_signal(barrier, inc=1, device_id=partner, device_id_type=MESH)
    pl.semaphore_signal(barrier, inc=1, device_id=core, device_id_type=MESH)

    @pl.when(has_left)
    def _():
        pl.semaphore_signal(barrier, inc=1, device_id=left, device_id_type=MESH)

    @pl.when(has_right)
    def _():
        pl.semaphore_signal(barrier, inc=1, device_id=right, device_id_type=MESH)

    between = has_left & has_right

    @pl.when(between)
    def _():
        pl.semaphore_wait(barrier, 4)

    @pl.when(jnp.logical_not(between))
    def _():
        pl.semaphore_wait(barrier, 3 if lines > 1 else 2)

    def kv_copy(step, slot, way):
        src = kv.at[step, slot]
        return pltpu.make_async_remote_copy(
            src_ref=src,
            dst_ref=kv.at[step, slot],
            send_sem=kv_send.at[step, slot, way],
            recv_sem=kv_recv.at[step, slot],
            device_id=(left, right)[way],
            device_id_type=MESH,
        )

    def start_own(step):
        @pl.when(has_left)
        def _():
            kv_copy(step, a, 0).start()

        @pl.when(has_right)
        def _():
            kv_copy(step, a, 1).start()

    def forward(step, k):
        @pl.when(a + k < lines)
        def _():
            kv_copy(step, a + k, 0).wait_recv()

            @pl.when(has_left)
            def _():
                kv_copy(step, a + k, 0).start()

        @pl.when(a - k >= 0)
        def _():
            kv_copy(step, a - k, 1).wait_recv()

            @pl.when(has_right)
            def _():
                kv_copy(step, a - k, 1).start()

    def drain(step):
        for k in range(lines):

            @pl.when((a + k < lines) & has_left)
            def _():
                kv_copy(step, a + k, 0).wait_send()

            @pl.when((a - k >= 0) & has_right)
            def _():
                kv_copy(step, a - k, 1).wait_send()

    def pair_copy(src, dst, sems, step, target):
        return pltpu.make_async_remote_copy(
            src_ref=src,
            dst_ref=dst,
            send_sem=sems.at[step, 0],
            recv_sem=sems.at[step, 1],
            device_id=target,
            device_id_type=MESH,
        )

    own_half = pl.ds(pl.multiple_of(head * rows, rows), rows)
    peer_half = pl.ds(pl.multiple_of((1 - head) * rows, rows), rows)

    def modulate(step, values):
        centre = jnp.mean(values, axis=-1, keepdims=True)
        shifted = values - centre
        spread = jnp.mean(jnp.square(shifted), axis=-1, keepdims=True)
        normed = shifted * lax.rsqrt(spread + EPS)
        scale = 1.0 + mod_ref[step, 0:1, :]
        hidden[step, own_half, :] = (normed * scale + mod_ref[step, 1:2, :]).astype(BF16)

    def rms(values):
        return values * lax.rsqrt(jnp.mean(jnp.square(values), axis=-1, keepdims=True) + EPS)

    def project(step, which, store):
        @pl.loop(0, heads // 2)
        def _(j):
            columns = pl.ds(pl.multiple_of(j * 2 * HD, 2 * HD), 2 * HD)
            out = jnp.dot(
                hidden[step], wqkv[which, :, columns], preferred_element_type=F32
            )
            store(2 * j, out[:, :HD])
            store(2 * j + 1, out[:, HD:])

    def weigh(queries, keys, values):
        scores = lax.dot_general(
            queries, keys, (((1,), (1,)), ((), ())), preferred_element_type=F32
        )
        weights = jnp.exp(scores).astype(BF16)
        extended = jnp.concatenate([values, jnp.ones_like(values)], axis=1)
        return jnp.dot(weights, extended, preferred_element_type=F32)

    def attend(step, slot):
        @pl.loop(0, heads)
        def _(h):
            keys, values = kv[step, slot, 0, h], kv[step, slot, 1, h]
            acc[1, h] += weigh(q_peer[step, h], keys, values)
            acc[0, h] += weigh(q_own[step, h], keys, values)

    def attend_blocks(step, k):
        @pl.when(a + k < lines)
        def _():
            attend(step, a + k)

        @pl.when(a - k >= 0)
        def _():
            attend(step, a - k)

    loads[3].start()
    for i in range(3):
        loads[i].start()
    loads[4].start()
    loads[3].wait()
    start_own(0)

    for step in range(STEPS):
        if step == 0:
            modulate(step, tokens_ref[...].astype(F32))
        hid = pair_copy(
            hidden.at[step, own_half], hidden.at[step, own_half], hid_sem, step, core
        )
        hid.start()
        hid.wait_recv()

        def store_query(h, out):
            q_own[step, h] = (rms(out) * HD ** (-0.5)).astype(BF16)

        def store_key(h, out):
            value = rms(out).astype(BF16)
            if step == 0:
                kv[1, a, 0, h] = value
            else:
                last_kv[0, h] = value

        def store_value(h, out):
            value = out.astype(BF16)
            if step == 0:
                kv[1, a, 1, h] = value
            else:
                last_kv[1, h] = value

        if step == 0:
            loads[0].wait()
        project(step, 0, store_query)
        queries = pair_copy(q_own.at[step], q_peer.at[step], q_sem, step, partner)
        queries.start()
        if step == 0:
            loads[1].wait()
        if step == 1:
            forward(step, 1)
        project(step, 1, store_key)
        if step == 0:
            loads[2].wait()
        project(step, 2, store_value)
        if step == 1:
            cache = pltpu.make_async_copy(last_kv, cache_hbm, load_sem.at[5])
            cache.start()
        forward(step, 1) if step == 0 else None
        queries.wait_recv()

        @pl.loop(0, heads)
        def _(h):
            acc[1, h] = weigh(q_peer[step, h], kv[step, a, 0, h], kv[step, a, 1, h])
            if step == 0:
                keys, values = kv[1, a, 0, h], kv[1, a, 1, h]
            else:
                keys, values = last_kv[0, h], last_kv[1, h]
            acc[0, h] = weigh(q_own[step, h], keys, values)

        for k in range(1, lines):
            if k > 1:
                forward(step, k)
            if step == 0 and k == max(1, lines - 2):
                start_own(1)
            attend_blocks(step, k)

        lane = lax.broadcasted_iota(jnp.int32, (size, HD), 1)
        packed = jnp.zeros((size, HD), F32)
        for h in range(heads):
            num_out[step, h] = acc[1, h, :, :HD].astype(BF16)
            packed = jnp.where(lane == h, acc[1, h, :, HD:], packed)
        den_out[step] = packed
        dens = pair_copy(den_out.at[step], den_in.at[step], den_sem, step, partner)
        nums = pair_copy(num_out.at[step], num_in.at[step], num_sem, step, partner)
        dens.start()
        nums.start()
        if step == 0:
            loads[4].wait()
        dens.wait_recv()
        nums.wait_recv()
        for h in range(heads):
            numerator = acc[0, h, :, :HD] + num_in[step, h].astype(F32)
            denominator = acc[0, h, :, HD:] + den_in[step, :, h : h + 1]
            attended[:, h * HD : (h + 1) * HD] = (numerator / denominator).astype(BF16)

        part_out[step] = jnp.dot(
            attended[peer_half, :], wout[...], preferred_element_type=F32
        ).astype(BF16)
        part = pair_copy(part_out.at[step], part_in.at[step], part_sem, step, core)
        part.start()
        mine = jnp.dot(attended[own_half, :], wout[...], preferred_element_type=F32)
        part.wait_recv()
        branch = mine + part_in[step].astype(F32)
        before = tokens_ref[...] if step == 0 else state[...]
        after = before.astype(F32) + (1.0 + mod_ref[step, 2:3, :]) * branch
        after = after.astype(BF16)
        if step + 1 < STEPS:
            state[...] = after
            modulate(step + 1, after.astype(F32))
        else:
            next_ref[...] = after
            cache.wait()
        hid.wait_send()
        queries.wait_send()
        dens.wait_send()
        nums.wait_send()
        part.wait_send()
        drain(step)


def body(tokens, stale_kv, qkv_weight, out_weight, modulation):
    rows, width = tokens.shape
    size, _, inner = stale_kv.shape
    heads = inner // HD
    lines = lax.axis_size("patch") // 2
    stale = stale_kv.reshape(size, 2, heads, HD).transpose(1, 2, 0, 3)
    vmem = pl.BlockSpec(memory_space=pltpu.VMEM)
    hbm = pl.BlockSpec(memory_space=pl.ANY)
    dma = pltpu.SemaphoreType.DMA
    next_tokens, cache = pl.pallas_call(
        functools.partial(kernel, lines),
        out_shape=(
            jax.ShapeDtypeStruct((rows, width), BF16),
            jax.ShapeDtypeStruct((2, heads, size, HD), BF16),
        ),
        in_specs=[vmem, hbm, hbm, hbm, vmem],
        out_specs=(vmem, hbm),
        scratch_shapes=[
            pltpu.VMEM((3, width, inner), BF16),
            pltpu.VMEM((inner, width), BF16),
            pltpu.VMEM((STEPS, lines, 2, heads, size, HD), BF16),
            pltpu.VMEM((2, heads, size, HD), BF16),
            pltpu.VMEM((STEPS, size, width), BF16),
            pltpu.VMEM((STEPS, heads, size, HD), BF16),
            pltpu.VMEM((STEPS, heads, size, HD), BF16),
            pltpu.VMEM((2, heads, size, 2 * HD), F32),
            pltpu.VMEM((STEPS, heads, size, HD), BF16),
            pltpu.VMEM((STEPS, heads, size, HD), BF16),
            pltpu.VMEM((STEPS, size, HD), F32),
            pltpu.VMEM((STEPS, size, HD), F32),
            pltpu.VMEM((size, inner), BF16),
            pltpu.VMEM((STEPS, rows, width), BF16),
            pltpu.VMEM((STEPS, rows, width), BF16),
            pltpu.VMEM((rows, width), BF16),
            dma((6,)),
            dma((STEPS, lines, 2)),
            dma((STEPS, lines)),
            dma((STEPS, 2)),
            dma((STEPS, 2)),
            dma((STEPS, 2)),
            dma((STEPS, 2)),
            dma((STEPS, 2)),
        ],
        compiler_params=pltpu.CompilerParams(
            collective_id=0, has_side_effects=True, vmem_limit_bytes=58 * 2**20
        ),
    )(tokens, stale, qkv_weight.transpose(1, 0, 2), out_weight, modulation)
    fresh = cache.transpose(2, 0, 1, 3).reshape(size, 2, inner)
    return next_tokens, fresh


def solution(mesh):
    in_specs = (
        P(("clips", "patch", "head"), None),
        P(("clips", "patch"), None, "head"),
        P(None, None, "head"),
        P("head", None),
        P(),
    )
    out_specs = (P(("clips", "patch", "head"), None), P(("clips", "patch"), None, "head"))
    return jax.shard_map(body, mesh=mesh, in_specs=in_specs, out_specs=out_specs, check_vma=False)
```

```python
import functools

import jax
import jax.numpy as jnp
from jax import lax
from jax.experimental import pallas as pl
from jax.experimental.pallas import tpu as pltpu
from jax.sharding import PartitionSpec as P

HD = 128
STEPS = 2
EPS = 1e-06
MESH = pl.DeviceIdType.MESH
F32, BF16 = jnp.float32, jnp.bfloat16


def kernel(
    lines,
    tokens_ref,
    stale_ref,
    wqkv_hbm,
    wout_hbm,
    mod_ref,
    next_ref,
    cache_hbm,
    wqkv,
    wout,
    kv,
    last_kv,
    hidden,
    q_own,
    q_peer,
    acc,
    q_help,
    help_acc,
    num_out,
    num_in,
    ret_out,
    ret_in,
    attended,
    part_out,
    part_in,
    state,
    load_sem,
    stale_sem,
    cache_sem,
    kv_send,
    kv_recv,
    hid_sem,
    q_sem,
    num_sem,
    help_sem,
    ret_sem,
    part_sem,
):
    patch, head = lax.axis_index("patch"), lax.axis_index("head")
    a, b = patch // 2, patch % 2
    rows = tokens_ref.shape[0]
    heads = q_own.shape[1]
    size = q_own.shape[2]
    half = heads // 2
    aided = lines >= 4
    left = {"patch": patch - 2, "head": head}
    right = {"patch": patch + 2, "head": head}
    partner = {"patch": a * 2 + (1 - b), "head": head}
    core = {"patch": patch, "head": 1 - head}
    has_left, has_right = a > 0, a < lines - 1

    loads = [
        pltpu.make_async_copy(wqkv_hbm.at[i], wqkv.at[i], load_sem.at[i]) for i in range(3)
    ]
    loads.append(pltpu.make_async_copy(wout_hbm, wout, load_sem.at[3]))
    stales = [
        pltpu.make_async_copy(
            stale_ref.at[i, :, h * HD : (h + 1) * HD], kv.at[0, a, i, h], stale_sem.at[i, h]
        )
        for i in range(2)
        for h in range(heads)
    ]
    caches = [
        pltpu.make_async_copy(
            last_kv.at[i, h], cache_hbm.at[i, :, h * HD : (h + 1) * HD], cache_sem.at[i, h]
        )
        for i in range(2)
        for h in range(heads)
    ]

    barrier = pltpu.get_barrier_semaphore()
    pl.semaphore_signal(barrier, inc=1, device_id=partner, device_id_type=MESH)
    pl.semaphore_signal(barrier, inc=1, device_id=core, device_id_type=MESH)

    @pl.when(has_left)
    def _():
        pl.semaphore_signal(barrier, inc=1, device_id=left, device_id_type=MESH)

    @pl.when(has_right)
    def _():
        pl.semaphore_signal(barrier, inc=1, device_id=right, device_id_type=MESH)

    between = has_left & has_right
    is_end = jnp.logical_not(between)
    if aided:
        is_helper = (a == 1) | (a == lines - 2)
        helper = {"patch": patch + 2 - 4 * (a // (lines - 1)), "head": head}
        aided_end = {"patch": patch - 2 + 4 * (a // (lines - 2)), "head": head}
    send_left = [has_left, a > 1 if aided else has_left]
    send_right = [has_right, a < lines - 2 if aided else has_right]

    def takes(group, present):
        return present & between if aided and group == 1 else present

    @pl.when(between)
    def _():
        pl.semaphore_wait(barrier, 4)

    @pl.when(jnp.logical_not(between))
    def _():
        pl.semaphore_wait(barrier, 3 if lines > 1 else 2)

    def kv_copy(step, slot, group, way):
        part = pl.ds(group * half, half)
        return pltpu.make_async_remote_copy(
            src_ref=kv.at[step, slot, :, part],
            dst_ref=kv.at[step, slot, :, part],
            send_sem=kv_send.at[step, slot, group, way],
            recv_sem=kv_recv.at[step, slot, group],
            device_id=(left, right)[way],
            device_id_type=MESH,
        )

    def start_own(step):
        for group in (1, 0):

            @pl.when(send_left[group])
            def _():
                kv_copy(step, a, group, 0).start()

            @pl.when(send_right[group])
            def _():
                kv_copy(step, a, group, 1).start()

    def forward(step, k, group):
        @pl.when(takes(group, a + k < lines))
        def _():
            kv_copy(step, a + k, group, 0).wait_recv()

            @pl.when(send_left[group])
            def _():
                kv_copy(step, a + k, group, 0).start()

        @pl.when(takes(group, a - k >= 0))
        def _():
            kv_copy(step, a - k, group, 1).wait_recv()

            @pl.when(send_right[group])
            def _():
                kv_copy(step, a - k, group, 1).start()

    def drain(step):
        for k in range(lines):
            for group in range(2):

                @pl.when((a + k < lines) & send_left[group])
                def _():
                    kv_copy(step, a + k, group, 0).wait_send()

                @pl.when((a - k >= 0) & send_right[group])
                def _():
                    kv_copy(step, a - k, group, 1).wait_send()

    def pair_copy(src, dst, sems, step, target, which=0):
        return pltpu.make_async_remote_copy(
            src_ref=src,
            dst_ref=dst,
            send_sem=sems.at[step, which, 0],
            recv_sem=sems.at[step, which, 1],
            device_id=target,
            device_id_type=MESH,
        )

    own_half = pl.ds(pl.multiple_of(head * rows, rows), rows)
    peer_half = pl.ds(pl.multiple_of((1 - head) * rows, rows), rows)

    def modulate(step, values):
        centre = jnp.mean(values, axis=-1, keepdims=True)
        shifted = values - centre
        spread = jnp.mean(jnp.square(shifted), axis=-1, keepdims=True)
        normed = shifted * lax.rsqrt(spread + EPS)
        scale = 1.0 + mod_ref[0, step : step + 1, :]
        hidden[step, own_half, :] = (normed * scale + mod_ref[1, step : step + 1, :]).astype(BF16)

    def rms(values):
        return values * lax.rsqrt(jnp.mean(jnp.square(values), axis=-1, keepdims=True) + EPS)

    def project(step, which, store):
        @pl.loop(0, heads // 2)
        def _(j):
            columns = pl.ds(pl.multiple_of(j * 2 * HD, 2 * HD), 2 * HD)
            out = jnp.dot(
                hidden[step], wqkv[which, :, columns], preferred_element_type=F32
            )
            store(2 * j, out[:, :HD])
            store(2 * j + 1, out[:, HD:])

    def weigh(queries, keys, values):
        scores = lax.dot_general(
            queries, keys, (((1,), (1,)), ((), ())), preferred_element_type=F32
        )
        weights = jnp.exp(scores).astype(BF16)
        extended = jnp.concatenate([values, jnp.ones_like(values)], axis=1)
        return jnp.dot(weights, extended, preferred_element_type=F32)

    def attend(step, slot, group):
        @pl.loop(group * half, (group + 1) * half)
        def _(h):
            keys, values = kv[step, slot, 0, h], kv[step, slot, 1, h]
            acc[1, h] += weigh(q_peer[step, h], keys, values)
            acc[0, h] += weigh(q_own[step, h], keys, values)

    def attend_blocks(step, k, group):
        @pl.when(takes(group, a + k < lines))
        def _():
            attend(step, a + k, group)

        @pl.when(takes(group, a - k >= 0))
        def _():
            attend(step, a - k, group)

    def aid(step, slot, first):
        @pl.loop(0, half)
        def _(h):
            keys, values = kv[step, slot, 0, half + h], kv[step, slot, 1, half + h]
            for i in range(2):
                sums = weigh(q_help[step, i, h], keys, values)
                help_acc[i, h] = sums if first else help_acc[i, h] + sums

    def aid_blocks(step, k):
        @pl.when((a == 1) & (a + k < lines))
        def _():
            aid(step, a + k, False)

        @pl.when((a == lines - 2) & (a - k >= 0))
        def _():
            aid(step, a - k, False)

    lane = lax.broadcasted_iota(jnp.int32, (size, HD), 1)

    def pack(totals):
        packed = jnp.zeros((size, HD), F32)
        for j, total in enumerate(totals):
            high = total.astype(BF16).astype(F32)
            packed = jnp.where(lane == j, high, packed)
            packed = jnp.where(lane == len(totals) + j, total - high, packed)
        return packed.astype(BF16)

    def unpack(packed, j, count):
        high = packed[:, j : j + 1].astype(F32)
        return high + packed[:, count + j : count + j + 1].astype(F32)

    for copy in stales:
        copy.start()
    for copy in loads:
        copy.start()
    for copy in stales:
        copy.wait()
    start_own(0)

    for step in range(STEPS):
        if step == 0:
            modulate(step, tokens_ref[...].astype(F32))
        hid = pair_copy(
            hidden.at[step, own_half], hidden.at[step, own_half], hid_sem, step, core
        )
        hid.start()
        hid.wait_recv()

        def store_query(h, out):
            q_own[step, h] = (rms(out) * HD ** (-0.5)).astype(BF16)

        def store_key(h, out):
            value = rms(out).astype(BF16)
            if step == 0:
                kv[1, a, 0, h] = value
            else:
                last_kv[0, h] = value

        def store_value(h, out):
            value = out.astype(BF16)
            if step == 0:
                kv[1, a, 1, h] = value
            else:
                last_kv[1, h] = value

        if step == 0:
            loads[0].wait()
        project(step, 0, store_query)
        queries = [
            pair_copy(
                q_own.at[step, pl.ds(g * half, half)],
                q_peer.at[step, pl.ds(g * half, half)],
                q_sem,
                step,
                partner,
                g,
            )
            for g in range(2)
        ]
        queries[1].start()
        queries[0].start()
        if aided:
            asks = [
                pair_copy(
                    source.at[step, pl.ds(half, half)],
                    q_help.at[step, i],
                    help_sem,
                    step,
                    helper,
                    i,
                )
                for i, source in enumerate((q_own, q_peer))
            ]
            answer = pair_copy(ret_out.at[step], ret_in.at[step], ret_sem, step, aided_end)

            @pl.when(is_end)
            def _():
                asks[0].start()

        if step == 0:
            loads[1].wait()
        if step == 1:
            forward(step, 1, 1)
            forward(step, 1, 0)
        project(step, 1, store_key)
        if step == 0:
            loads[2].wait()
        project(step, 2, store_value)
        if step == 1:
            for copy in caches:
                copy.start()
        queries[1].wait_recv()
        if aided:

            @pl.when(is_end)
            def _():
                asks[1].start()

        if step == 0:
            forward(step, 1, 1)
            forward(step, 1, 0)
        queries[0].wait_recv()

        @pl.loop(0, heads)
        def _(h):
            acc[1, h] = weigh(q_peer[step, h], kv[step, a, 0, h], kv[step, a, 1, h])
            if step == 0:
                keys, values = kv[1, a, 0, h], kv[1, a, 1, h]
            else:
                keys, values = last_kv[0, h], last_kv[1, h]
            acc[0, h] = weigh(q_own[step, h], keys, values)

        if aided:

            @pl.when(is_helper)
            def _():
                asks[0].wait_recv()
                asks[1].wait_recv()
                aid(step, a, True)

        nums = [
            pair_copy(num_out.at[step, g], num_in.at[step, g], num_sem, step, partner, g)
            for g in range(2)
        ]

        def send_sums(group):
            for h in range(half):
                num_out[step, group, h] = acc[1, group * half + h, :, :HD].astype(BF16)
            num_out[step, group, half] = pack(
                [acc[1, group * half + h, :, HD:] for h in range(half)]
            )
            nums[group].start()

        for k in range(1, lines):
            for group in (1, 0):
                if k > 1:
                    forward(step, k, group)
                attend_blocks(step, k, group)
                if aided and group == 1:
                    aid_blocks(step, k)
                    if k == lines - 2:

                        @pl.when(is_helper)
                        def _():
                            for i in range(2):
                                for h in range(half):
                                    ret_out[step, i * half + h] = help_acc[
                                        i, h, :, :HD
                                    ].astype(BF16)
                            ret_out[step, heads] = pack(
                                [help_acc[i, h, :, HD:] for i in range(2) for h in range(half)]
                            )
                            answer.start()

                if group == 1 and k == lines - 1:
                    if aided:

                        @pl.when(between)
                        def _():
                            send_sums(1)

                    else:
                        send_sums(1)
            if step == 0 and k == max(1, lines - 2):
                start_own(1)
        send_sums(0)
        if aided:

            @pl.when(is_end)
            def _():
                answer.wait_recv()
                for i in range(2):
                    for h in range(half):
                        j = i * half + h
                        acc[i, half + h, :, :HD] += ret_in[step, j].astype(F32)
                        acc[i, half + h, :, HD:] += unpack(ret_in[step, heads], j, heads)
                send_sums(1)

        if step == 0:
            loads[3].wait()
        for group in range(2):
            nums[group].wait_recv()
            for j in range(half):
                h = group * half + j
                numerator = acc[0, h, :, :HD] + num_in[step, group, j].astype(F32)
                denominator = acc[0, h, :, HD:] + unpack(num_in[step, group, half], j, half)
                attended[:, h * HD : (h + 1) * HD] = (numerator / denominator).astype(BF16)

        part_out[step] = jnp.dot(
            attended[peer_half, :], wout[...], preferred_element_type=F32
        ).astype(BF16)
        part = pair_copy(part_out.at[step], part_in.at[step], part_sem, step, core)
        part.start()
        mine = jnp.dot(attended[own_half, :], wout[...], preferred_element_type=F32)
        part.wait_recv()
        branch = mine + part_in[step].astype(F32)
        before = tokens_ref[...] if step == 0 else state[...]
        after = before.astype(F32) + (1.0 + mod_ref[2, step : step + 1, :]) * branch
        after = after.astype(BF16)
        if step + 1 < STEPS:
            state[...] = after
            modulate(step + 1, after.astype(F32))
        else:
            next_ref[...] = after
            for copy in caches:
                copy.wait()
        hid.wait_send()
        part.wait_send()
        for group in range(2):
            queries[group].wait_send()
            nums[group].wait_send()
        if aided:

            @pl.when(is_end)
            def _():
                asks[0].wait_send()
                asks[1].wait_send()

            @pl.when(is_helper)
            def _():
                answer.wait_send()

        drain(step)


def body(tokens, stale_kv, qkv_weight, out_weight, modulation):
    rows, width = tokens.shape
    size, _, inner = stale_kv.shape
    heads = inner // HD
    lines = lax.axis_size("patch") // 2
    stale = stale_kv.transpose(1, 0, 2)
    vmem = pl.BlockSpec(memory_space=pltpu.VMEM)
    hbm = pl.BlockSpec(memory_space=pl.ANY)
    dma = pltpu.SemaphoreType.DMA
    next_tokens, cache = pl.pallas_call(
        functools.partial(kernel, lines),
        out_shape=(
            jax.ShapeDtypeStruct((rows, width), BF16),
            jax.ShapeDtypeStruct((2, size, inner), BF16),
        ),
        in_specs=[vmem, hbm, hbm, hbm, vmem],
        out_specs=(vmem, hbm),
        scratch_shapes=[
            pltpu.VMEM((3, width, inner), BF16),
            pltpu.VMEM((inner, width), BF16),
            pltpu.VMEM((STEPS, lines, 2, heads, size, HD), BF16),
            pltpu.VMEM((2, heads, size, HD), BF16),
            pltpu.VMEM((STEPS, size, width), BF16),
            pltpu.VMEM((STEPS, heads, size, HD), BF16),
            pltpu.VMEM((STEPS, heads, size, HD), BF16),
            pltpu.VMEM((2, heads, size, 2 * HD), F32),
            pltpu.VMEM((STEPS, 2, heads // 2, size, HD), BF16),
            pltpu.VMEM((2, heads // 2, size, 2 * HD), F32),
            pltpu.VMEM((STEPS, 2, heads // 2 + 1, size, HD), BF16),
            pltpu.VMEM((STEPS, 2, heads // 2 + 1, size, HD), BF16),
            pltpu.VMEM((STEPS, heads + 1, size, HD), BF16),
            pltpu.VMEM((STEPS, heads + 1, size, HD), BF16),
            pltpu.VMEM((size, inner), BF16),
            pltpu.VMEM((STEPS, rows, width), BF16),
            pltpu.VMEM((STEPS, rows, width), BF16),
            pltpu.VMEM((rows, width), BF16),
            dma((4,)),
            dma((2, heads)),
            dma((2, heads)),
            dma((STEPS, lines, 2, 2)),
            dma((STEPS, lines, 2)),
            dma((STEPS, 1, 2)),
            dma((STEPS, 2, 2)),
            dma((STEPS, 2, 2)),
            dma((STEPS, 2, 2)),
            dma((STEPS, 1, 2)),
            dma((STEPS, 1, 2)),
        ],
        compiler_params=pltpu.CompilerParams(
            collective_id=0, has_side_effects=True, vmem_limit_bytes=58 * 2**20
        ),
    )(tokens, stale, qkv_weight.transpose(1, 0, 2), out_weight, modulation.transpose(1, 0, 2))
    return next_tokens, cache.transpose(1, 0, 2)


def solution(mesh):
    in_specs = (
        P(("clips", "patch", "head"), None),
        P(("clips", "patch"), None, "head"),
        P(None, None, "head"),
        P("head", None),
        P(),
    )
    out_specs = (P(("clips", "patch", "head"), None), P(("clips", "patch"), None, "head"))
    return jax.shard_map(body, mesh=mesh, in_specs=in_specs, out_specs=out_specs, check_vma=False)
```

```python
import functools

import jax
import jax.numpy as jnp
from jax import lax
from jax.experimental import pallas as pl
from jax.experimental.pallas import tpu as pltpu
from jax.sharding import PartitionSpec as P

HD = 128
STEPS = 2
EPS = 1e-06
MESH = pl.DeviceIdType.MESH
F32, BF16 = jnp.float32, jnp.bfloat16


def kernel(
    lines,
    tokens_ref,
    stale_ref,
    wqkv_hbm,
    wout_hbm,
    mod_ref,
    next_ref,
    cache_hbm,
    wqkv,
    wout,
    kv,
    last_kv,
    hidden,
    q_own,
    q_peer,
    acc,
    q_help,
    help_acc,
    num_out,
    num_in,
    ret_out,
    ret_in,
    attended,
    part_out,
    part_in,
    state,
    load_sem,
    stale_sem,
    cache_sem,
    kv_send,
    kv_recv,
    hid_sem,
    q_sem,
    num_sem,
    help_sem,
    ret_sem,
    part_sem,
):
    patch, head = lax.axis_index("patch"), lax.axis_index("head")
    a, b = patch // 2, patch % 2
    rows = tokens_ref.shape[0]
    heads = q_own.shape[1]
    size = q_own.shape[2]
    half = heads // 2
    aid_steps = [lines >= 4, False]
    left = {"patch": patch - 2, "head": head}
    right = {"patch": patch + 2, "head": head}
    partner = {"patch": a * 2 + (1 - b), "head": head}
    core = {"patch": patch, "head": 1 - head}
    has_left, has_right = a > 0, a < lines - 1

    loads = [
        pltpu.make_async_copy(wqkv_hbm.at[i], wqkv.at[i], load_sem.at[i]) for i in range(3)
    ]
    loads.append(pltpu.make_async_copy(wout_hbm, wout, load_sem.at[3]))
    stales = [
        pltpu.make_async_copy(
            stale_ref.at[i, :, h * HD : (h + 1) * HD], kv.at[0, a, i, h], stale_sem.at[i, h]
        )
        for i in range(2)
        for h in range(heads)
    ]
    caches = [
        pltpu.make_async_copy(
            last_kv.at[i, h], cache_hbm.at[i, :, h * HD : (h + 1) * HD], cache_sem.at[i, h]
        )
        for i in range(2)
        for h in range(heads)
    ]

    barrier = pltpu.get_barrier_semaphore()
    pl.semaphore_signal(barrier, inc=1, device_id=partner, device_id_type=MESH)
    pl.semaphore_signal(barrier, inc=1, device_id=core, device_id_type=MESH)

    @pl.when(has_left)
    def _():
        pl.semaphore_signal(barrier, inc=1, device_id=left, device_id_type=MESH)

    @pl.when(has_right)
    def _():
        pl.semaphore_signal(barrier, inc=1, device_id=right, device_id_type=MESH)

    between = has_left & has_right
    is_end = jnp.logical_not(between)
    if any(aid_steps):
        is_helper = (a == 1) | (a == lines - 2)
        helper = {"patch": patch + 2 - 4 * (a // (lines - 1)), "head": head}
        aided_end = {"patch": patch - 2 + 4 * (a // (lines - 2)), "head": head}
    send_left, send_right = [], []
    for aided in aid_steps:
        send_left.append([has_left, a > 1 if aided else has_left])
        send_right.append([has_right, a < lines - 2 if aided else has_right])

    def takes(step, group, present):
        return present & between if aid_steps[step] and group == 1 else present

    @pl.when(between)
    def _():
        pl.semaphore_wait(barrier, 4)

    @pl.when(jnp.logical_not(between))
    def _():
        pl.semaphore_wait(barrier, 3 if lines > 1 else 2)

    def kv_copy(step, slot, group, way):
        part = pl.ds(group * half, half)
        return pltpu.make_async_remote_copy(
            src_ref=kv.at[step, slot, :, part],
            dst_ref=kv.at[step, slot, :, part],
            send_sem=kv_send.at[step, slot, group, way],
            recv_sem=kv_recv.at[step, slot, group],
            device_id=(left, right)[way],
            device_id_type=MESH,
        )

    def start_own(step, leftward, rightward):
        for group in (1, 0):

            @pl.when(send_left[step][group] & leftward)
            def _():
                kv_copy(step, a, group, 0).start()

            @pl.when(send_right[step][group] & rightward)
            def _():
                kv_copy(step, a, group, 1).start()

    def forward(step, k, group):
        @pl.when(takes(step, group, a + k < lines))
        def _():
            kv_copy(step, a + k, group, 0).wait_recv()

            @pl.when(send_left[step][group])
            def _():
                kv_copy(step, a + k, group, 0).start()

        @pl.when(takes(step, group, a - k >= 0))
        def _():
            kv_copy(step, a - k, group, 1).wait_recv()

            @pl.when(send_right[step][group])
            def _():
                kv_copy(step, a - k, group, 1).start()

    def drain(step):
        for k in range(lines):
            for group in range(2):

                @pl.when((a + k < lines) & send_left[step][group])
                def _():
                    kv_copy(step, a + k, group, 0).wait_send()

                @pl.when((a - k >= 0) & send_right[step][group])
                def _():
                    kv_copy(step, a - k, group, 1).wait_send()

    def pair_copy(src, dst, sems, step, target, which=0):
        return pltpu.make_async_remote_copy(
            src_ref=src,
            dst_ref=dst,
            send_sem=sems.at[step, which, 0],
            recv_sem=sems.at[step, which, 1],
            device_id=target,
            device_id_type=MESH,
        )

    own_half = pl.ds(pl.multiple_of(head * rows, rows), rows)
    peer_half = pl.ds(pl.multiple_of((1 - head) * rows, rows), rows)

    def modulate(step, values):
        centre = jnp.mean(values, axis=-1, keepdims=True)
        shifted = values - centre
        spread = jnp.mean(jnp.square(shifted), axis=-1, keepdims=True)
        normed = shifted * lax.rsqrt(spread + EPS)
        scale = 1.0 + mod_ref[0, step : step + 1, :]
        hidden[step, own_half, :] = (normed * scale + mod_ref[1, step : step + 1, :]).astype(BF16)

    def rms(values):
        return values * lax.rsqrt(jnp.mean(jnp.square(values), axis=-1, keepdims=True) + EPS)

    def project(step, which, store):
        @pl.loop(0, heads // 2)
        def _(j):
            columns = pl.ds(pl.multiple_of(j * 2 * HD, 2 * HD), 2 * HD)
            out = jnp.dot(
                hidden[step], wqkv[which, :, columns], preferred_element_type=F32
            )
            store(2 * j, out[:, :HD])
            store(2 * j + 1, out[:, HD:])

    def weigh(queries, keys, values):
        scores = lax.dot_general(
            queries, keys, (((1,), (1,)), ((), ())), preferred_element_type=F32
        )
        weights = jnp.exp(scores).astype(BF16)
        extended = jnp.concatenate([values, jnp.ones_like(values)], axis=1)
        return jnp.dot(weights, extended, preferred_element_type=F32)

    def attend(step, slot, group):
        @pl.loop(group * half, (group + 1) * half)
        def _(h):
            keys, values = kv[step, slot, 0, h], kv[step, slot, 1, h]
            acc[1, h] += weigh(q_peer[step, h], keys, values)
            acc[0, h] += weigh(q_own[step, h], keys, values)

    def attend_blocks(step, k, group):
        @pl.when(takes(step, group, a + k < lines))
        def _():
            attend(step, a + k, group)

        @pl.when(takes(step, group, a - k >= 0))
        def _():
            attend(step, a - k, group)

    def aid(step, slot, first):
        @pl.loop(0, half)
        def _(h):
            keys, values = kv[step, slot, 0, half + h], kv[step, slot, 1, half + h]
            for i in range(2):
                sums = weigh(q_help[step, i, h], keys, values)
                help_acc[i, h] = sums if first else help_acc[i, h] + sums

    def aid_blocks(step, k):
        @pl.when((a == 1) & (a + k < lines))
        def _():
            aid(step, a + k, False)

        @pl.when((a == lines - 2) & (a - k >= 0))
        def _():
            aid(step, a - k, False)

    lane = lax.broadcasted_iota(jnp.int32, (size, HD), 1)

    def pack(totals):
        packed = jnp.zeros((size, HD), F32)
        for j, total in enumerate(totals):
            high = total.astype(BF16).astype(F32)
            packed = jnp.where(lane == j, high, packed)
            packed = jnp.where(lane == len(totals) + j, total - high, packed)
        return packed.astype(BF16)

    def unpack(packed, j, count):
        high = packed[:, j : j + 1].astype(F32)
        return high + packed[:, count + j : count + j + 1].astype(F32)

    for copy in stales:
        copy.start()
    for copy in loads:
        copy.start()
    for copy in stales:
        copy.wait()
    start_own(0, a >= 0, a >= 0)

    early_left = (a == lines - 1) | (a == 1)
    early_right = (a == 0) | (a == lines - 2)

    for step in range(STEPS):
        aided = aid_steps[step]
        if step == 0:
            modulate(step, tokens_ref[...].astype(F32))
        hid = pair_copy(
            hidden.at[step, own_half], hidden.at[step, own_half], hid_sem, step, core
        )
        hid.start()
        hid.wait_recv()

        def store_query(h, out):
            q_own[step, h] = (rms(out) * HD ** (-0.5)).astype(BF16)

        def store_key(h, out):
            value = rms(out).astype(BF16)
            if step == 0:
                kv[1, a, 0, h] = value
            else:
                last_kv[0, h] = value

        def store_value(h, out):
            value = out.astype(BF16)
            if step == 0:
                kv[1, a, 1, h] = value
            else:
                last_kv[1, h] = value

        if step == 0:
            loads[0].wait()
        project(step, 0, store_query)
        queries = [
            pair_copy(
                q_own.at[step, pl.ds(g * half, half)],
                q_peer.at[step, pl.ds(g * half, half)],
                q_sem,
                step,
                partner,
                g,
            )
            for g in range(2)
        ]
        queries[1].start()
        queries[0].start()
        if aided:
            asks = [
                pair_copy(
                    source.at[step, pl.ds(half, half)],
                    q_help.at[step, i],
                    help_sem,
                    step,
                    helper,
                    i,
                )
                for i, source in enumerate((q_own, q_peer))
            ]
            answer = pair_copy(ret_out.at[step], ret_in.at[step], ret_sem, step, aided_end)

            @pl.when(is_end)
            def _():
                asks[0].start()

        if step == 0:
            loads[1].wait()
        project(step, 1, store_key)
        if step == 0:
            loads[2].wait()
        project(step, 2, store_value)
        if step == 1:
            for copy in caches:
                copy.start()
        queries[1].wait_recv()
        if aided:

            @pl.when(is_end)
            def _():
                asks[1].start()

        if step == 0:
            forward(step, 1, 1)
            forward(step, 1, 0)
            start_own(1, early_left, early_right)
        queries[0].wait_recv()

        @pl.loop(0, heads)
        def _(h):
            acc[1, h] = weigh(q_peer[step, h], kv[step, a, 0, h], kv[step, a, 1, h])
            if step == 0:
                keys, values = kv[1, a, 0, h], kv[1, a, 1, h]
            else:
                keys, values = last_kv[0, h], last_kv[1, h]
            acc[0, h] = weigh(q_own[step, h], keys, values)

        nums = [
            pair_copy(num_out.at[step, g], num_in.at[step, g], num_sem, step, partner, g)
            for g in range(2)
        ]

        def send_sums(group):
            for h in range(half):
                num_out[step, group, h] = acc[1, group * half + h, :, :HD].astype(BF16)
            num_out[step, group, half] = pack(
                [acc[1, group * half + h, :, HD:] for h in range(half)]
            )
            nums[group].start()

        for k in range(1, lines):
            for group in (1, 0):
                if k > 1:
                    forward(step, k, group)
                attend_blocks(step, k, group)
                if group == 1 and k == lines - 1:
                    if aided:

                        @pl.when(between)
                        def _():
                            send_sums(1)

                    else:
                        send_sums(1)
            if step == 0 and k == max(1, lines - 2):
                start_own(1, jnp.logical_not(early_left), jnp.logical_not(early_right))
        send_sums(0)
        if aided:

            @pl.when(is_helper)
            def _():
                asks[0].wait_recv()
                asks[1].wait_recv()
                aid(step, a, True)
                for k in range(1, lines):
                    aid_blocks(step, k)
                for i in range(2):
                    for h in range(half):
                        ret_out[step, i * half + h] = help_acc[i, h, :, :HD].astype(BF16)
                ret_out[step, heads] = pack(
                    [help_acc[i, h, :, HD:] for i in range(2) for h in range(half)]
                )
                answer.start()

            @pl.when(is_end)
            def _():
                answer.wait_recv()
                for i in range(2):
                    for h in range(half):
                        j = i * half + h
                        acc[i, half + h, :, :HD] += ret_in[step, j].astype(F32)
                        acc[i, half + h, :, HD:] += unpack(ret_in[step, heads], j, heads)
                send_sums(1)

        if step == 0:
            loads[3].wait()
        for group in range(2):
            nums[group].wait_recv()
            for j in range(half):
                h = group * half + j
                numerator = acc[0, h, :, :HD] + num_in[step, group, j].astype(F32)
                denominator = acc[0, h, :, HD:] + unpack(num_in[step, group, half], j, half)
                attended[:, h * HD : (h + 1) * HD] = (numerator / denominator).astype(BF16)

        part_out[step] = jnp.dot(
            attended[peer_half, :], wout[...], preferred_element_type=F32
        ).astype(BF16)
        part = pair_copy(part_out.at[step], part_in.at[step], part_sem, step, core)
        part.start()
        if step == 0:
            forward(1, 1, 1)
            forward(1, 1, 0)
        mine = jnp.dot(attended[own_half, :], wout[...], preferred_element_type=F32)
        part.wait_recv()
        branch = mine + part_in[step].astype(F32)
        before = tokens_ref[...] if step == 0 else state[...]
        after = before.astype(F32) + (1.0 + mod_ref[2, step : step + 1, :]) * branch
        after = after.astype(BF16)
        if step + 1 < STEPS:
            state[...] = after
            modulate(step + 1, after.astype(F32))
        else:
            next_ref[...] = after
            for copy in caches:
                copy.wait()
        hid.wait_send()
        part.wait_send()
        for group in range(2):
            queries[group].wait_send()
            nums[group].wait_send()
        if aided:

            @pl.when(is_end)
            def _():
                asks[0].wait_send()
                asks[1].wait_send()

            @pl.when(is_helper)
            def _():
                answer.wait_send()

        drain(step)


def body(tokens, stale_kv, qkv_weight, out_weight, modulation):
    rows, width = tokens.shape
    size, _, inner = stale_kv.shape
    heads = inner // HD
    lines = lax.axis_size("patch") // 2
    stale = stale_kv.transpose(1, 0, 2)
    vmem = pl.BlockSpec(memory_space=pltpu.VMEM)
    hbm = pl.BlockSpec(memory_space=pl.ANY)
    dma = pltpu.SemaphoreType.DMA
    next_tokens, cache = pl.pallas_call(
        functools.partial(kernel, lines),
        out_shape=(
            jax.ShapeDtypeStruct((rows, width), BF16),
            jax.ShapeDtypeStruct((2, size, inner), BF16),
        ),
        in_specs=[vmem, hbm, hbm, hbm, vmem],
        out_specs=(vmem, hbm),
        scratch_shapes=[
            pltpu.VMEM((3, width, inner), BF16),
            pltpu.VMEM((inner, width), BF16),
            pltpu.VMEM((STEPS, lines, 2, heads, size, HD), BF16),
            pltpu.VMEM((2, heads, size, HD), BF16),
            pltpu.VMEM((STEPS, size, width), BF16),
            pltpu.VMEM((STEPS, heads, size, HD), BF16),
            pltpu.VMEM((STEPS, heads, size, HD), BF16),
            pltpu.VMEM((2, heads, size, 2 * HD), F32),
            pltpu.VMEM((STEPS, 2, heads // 2, size, HD), BF16),
            pltpu.VMEM((2, heads // 2, size, 2 * HD), F32),
            pltpu.VMEM((STEPS, 2, heads // 2 + 1, size, HD), BF16),
            pltpu.VMEM((STEPS, 2, heads // 2 + 1, size, HD), BF16),
            pltpu.VMEM((STEPS, heads + 1, size, HD), BF16),
            pltpu.VMEM((STEPS, heads + 1, size, HD), BF16),
            pltpu.VMEM((size, inner), BF16),
            pltpu.VMEM((STEPS, rows, width), BF16),
            pltpu.VMEM((STEPS, rows, width), BF16),
            pltpu.VMEM((rows, width), BF16),
            dma((4,)),
            dma((2, heads)),
            dma((2, heads)),
            dma((STEPS, lines, 2, 2)),
            dma((STEPS, lines, 2)),
            dma((STEPS, 1, 2)),
            dma((STEPS, 2, 2)),
            dma((STEPS, 2, 2)),
            dma((STEPS, 2, 2)),
            dma((STEPS, 1, 2)),
            dma((STEPS, 1, 2)),
        ],
        compiler_params=pltpu.CompilerParams(
            collective_id=0, has_side_effects=True, vmem_limit_bytes=58 * 2**20
        ),
    )(tokens, stale, qkv_weight.transpose(1, 0, 2), out_weight, modulation.transpose(1, 0, 2))
    return next_tokens, cache.transpose(1, 0, 2)


def solution(mesh):
    in_specs = (
        P(("clips", "patch", "head"), None),
        P(("clips", "patch"), None, "head"),
        P(None, None, "head"),
        P("head", None),
        P(),
    )
    out_specs = (P(("clips", "patch", "head"), None), P(("clips", "patch"), None, "head"))
    return jax.shard_map(body, mesh=mesh, in_specs=in_specs, out_specs=out_specs, check_vma=False)
```
